32 devices in a mesh: dp: 8 (over y, x, core), tp: 4 (over z).
Axes of the slice: x: 2, y: 2, z: 4, core: 2. Of those that a mesh axis runs over, the one named last changes fastest.
Arguments:
- queries: bfloat16 [512, 4, 64, 128], P('dp', None, 'tp'), may hold values from -6 to 6
- new_keys: bfloat16 [512, 4, 8, 128], P('dp', None, 'tp'), may hold values from -6 to 6
- new_values: bfloat16 [512, 4, 8, 128], P('dp', None, 'tp'), may hold values from -6 to 6
- suffix_keys: bfloat16 [512, 256, 8, 128], P('dp', None, 'tp'), may hold values from -6 to 6
- suffix_values: bfloat16 [512, 256, 8, 128], P('dp', None, 'tp'), may hold values from -6 to 6
- suffix_lengths: int32 [512], P('dp'), may hold values from 1 to 256
- prefix_ids: int32 [512, 1], P('dp'), may hold values from 0 to 7; in each aligned block of 64 rows (0 to 63, 64 to 127, ...) at most 16 rows name the same one
- prefix_owner: int32 [8], replicated, may hold values from 0 to 7, each once
- prefix_keys: bfloat16 [8, 2048, 8, 128], P('dp', None, 'tp'), may hold values from -6 to 6
- prefix_values: bfloat16 [8, 2048, 8, 128], P('dp', None, 'tp'), may hold values from -6 to 6
Outputs:
- attended: bfloat16 [512, 4, 64, 128], P('dp', None, 'tp')
The draws below stay inside these ranges and needn't reach their ends.
Inputs may be any that keep to these rules, and one draw needn't show every extreme that they name: `prefix_ids`: in each aligned block of 64 rows (the rows of one dp index) no prefix is named by more than 16 rows. `prefix_owner`: each dp index stores exactly one prefix.
All inputs are finite; a program needn't handle non-finite values.
Results may differ from the reference program's by a relative error of at most 0.0048.
Values may be sent and summed in bfloat16 or wider, within the bound.
A program may use at most 128 MiB of HBM per device.

```python
import math
import jax
import jax.numpy as jnp
import numpy as np
from jax import lax

HD = 128
QH = 64
KVH = 8
R_DEV = 64
STEPS = 4
PLEN = 2048
SLEN = 256
GQ = 8
CAP = 16
REQS = 512
PREFIXES = 8
N_DP = 8


def draw_queries(key, part):
    key = jax.random.fold_in(key, 11)
    first_key = jax.random.fold_in(key, 0)
    values = jnp.clip(jax.random.normal(first_key, (REQS, STEPS, QH, HD), jnp.float32), -6.0, 6.0)
    return values.astype(jnp.bfloat16)


def draw_prefix_keys(key, part):
    key = jax.random.fold_in(key, 12)
    first_key = jax.random.fold_in(key, 0)
    values = jnp.clip(jax.random.normal(first_key, (N_DP, PLEN, KVH, HD), jnp.float32), -6.0, 6.0)
    return values.astype(jnp.bfloat16)


def draw_suffix_lengths(key, part):
    key = jax.random.fold_in(key, 13)
    first_key, second_key = jax.random.split(key)
    lengths = jax.random.randint(first_key, (REQS,), 1, SLEN + 1)
    spot = jax.random.randint(second_key, (), 0, REQS)
    return jnp.where(jnp.arange(REQS) == spot, SLEN, lengths).astype(jnp.int32)


def block_scale(rng, extent, pieces, smallest, high):
    gain, own = 1.0, jax.random.fold_in(rng, 6)
    for dim, parts in pieces:
        steps = jnp.exp(jax.random.uniform(jax.random.fold_in(own, dim), (parts,), jnp.float32, smallest / len(pieces), high / len(pieces)))
        gain = gain * jnp.repeat(steps, extent[dim] // parts).reshape([-1 if axis == dim else 1 for axis in range(len(extent))])
    return gain


def routed_block(stream_key, own, number, rows, number_of, top, most, skew):
    order = jax.random.permutation(stream_key, number_of)
    heavy_load, usual = shares(number_of, rows * top, most, skew, True), shares(number_of, rows * top, most, skew, False)
    places = jnp.arange(number_of)

    def named(tallies, offset_by):
        used = int((tallies > 0).sum())
        fixed = max(1, used // 4)
        moved = fixed + (places - fixed + offset_by * (used - fixed)) % max(1, number_of - fixed)
        return jnp.zeros((number_of,), jnp.int32).at[order[jnp.where(places < fixed, places, moved)]].set(jnp.asarray(tallies, jnp.int32))

    tallies = jnp.where(number % 4 == 0, named(heavy_load, number // 4), named(usual, number - number // 4 - 1))
    mixed = jax.random.permutation(jax.random.fold_in(own, 3), number_of)
    donor, receiver = mixed[0:number_of // 2 * 2:2], mixed[1:number_of // 2 * 2:2]
    slack = jnp.minimum(tallies[donor] - 1, most - tallies[receiver]) // 2
    slack = jnp.where((donor == order[0]) | (receiver == order[0]) | (tallies[receiver] == 0), 0, jnp.maximum(slack, 0))
    moved = jax.random.randint(jax.random.fold_in(own, 4), (number_of // 2,), 0, 1 << 20) % (slack + 1)
    tallies = tallies.at[donor].add(-moved).at[receiver].add(moved)
    items = jnp.searchsorted(jnp.cumsum(tallies), jnp.arange(rows * top), side="right").astype(jnp.int32)
    table = items.reshape(top, rows).T
    table = table[jax.random.permutation(jax.random.fold_in(own, 1), rows)]
    offset_by = jax.random.randint(jax.random.fold_in(own, 2), (rows, 1), 0, top)
    return jnp.take_along_axis(table, (jnp.arange(top)[None, :] + offset_by) % top, axis=1)


def shares(amount, total, bound, slope, full):
    loads = [(1 << 20) // math.isqrt(standing ** slope) + 1 for standing in range(1, amount + 1)]
    largest = bound if full else min(bound, max(-(-total // amount), total * loads[0] // sum(loads)))
    least = 1 if total - largest >= amount - 1 else 0
    counts, spare = [largest] + [least] * (amount - 1), total - largest - least * (amount - 1)
    while spare > 0:
        movable = [i for i in range(1, amount) if counts[i] < largest] or [i for i in range(1, amount) if counts[i] < bound]
        whole, budget = sum([loads[i] for i in movable]), spare
        for i in movable:
            extra = min(bound - counts[i], max(1, budget * loads[i] // whole), spare)
            counts[i] = counts[i] + extra
            spare = spare - extra
    return np.array(counts)


def centred(key, shape, spread, bound, cuts=(), held_as=jnp.bfloat16):
    entries = jax.random.normal(key, shape, jnp.float32) * spread
    if len(cuts) > 0:
        entries = block_scale(key, shape, cuts, -0.22, 0.18) * entries
    return jnp.clip(entries, min=-bound, max=bound).astype(held_as)


def setup_inputs(seed: int = 0) -> dict:
    seeds = jax.random.split(jax.random.key(seed), 11)
    queries = draw_queries(jax.random.fold_in(seeds[10], 71), 0)
    new_keys = centred(seeds[1], (REQS, STEPS, KVH, HD), 2.0, 6.0, ((0, 8), (2, 4)))
    new_values = centred(seeds[2], (REQS, STEPS, KVH, HD), 1.0, 6.0, ((0, 8), (2, 4)))
    suffix_keys = centred(seeds[3], (REQS, SLEN, KVH, HD), 1.0, 6.0, ((0, 8), (2, 4)))
    suffix_values = centred(seeds[4], (REQS, SLEN, KVH, HD), 1.0, 6.0, ((0, 8), (2, 4)))
    suffix_lengths = draw_suffix_lengths(jax.random.fold_in(seeds[10], 71), 0)
    prefix_ids_keys = jax.random.split(jax.random.fold_in(seeds[6], 1), REQS // R_DEV)
    prefix_ids_turns = jax.random.permutation(jax.random.fold_in(seeds[6], 3), REQS // R_DEV)
    prefix_ids = jax.vmap(lambda own, number: routed_block(jax.random.fold_in(seeds[6], 2), own, number, R_DEV, PREFIXES, 1, CAP, 2))(prefix_ids_keys, prefix_ids_turns).reshape((REQS, 1))
    prefix_owner = jax.random.permutation(seeds[7], N_DP).astype(jnp.int32)
    prefix_keys = draw_prefix_keys(jax.random.fold_in(seeds[10], 71), 0)
    prefix_values = centred(seeds[9], (N_DP, PLEN, KVH, HD), 1.0, 6.0, ((0, 8), (2, 4)))
    return {"queries": queries, "new_keys": new_keys, "new_values": new_values, "suffix_keys": suffix_keys, "suffix_values": suffix_values, "suffix_lengths": suffix_lengths, "prefix_ids": prefix_ids, "prefix_owner": prefix_owner, "prefix_keys": prefix_keys, "prefix_values": prefix_values}


NEGATIVE = -1e30


def rounded(weights):
    return lax.optimization_barrier(weights.astype(jnp.bfloat16)).astype(jnp.float32)


def prefix_partial(grouped, cache_keys, cache_values):
    scores = jnp.einsum("rskgd,rpkd->rskgp", grouped.astype(jnp.float32), cache_keys.astype(jnp.float32)) * (HD ** -0.5)
    highest = jnp.max(scores, axis=-1)
    weights = jnp.exp(scores - highest[..., None])
    total = jnp.sum(weights, axis=-1)
    summed = jnp.einsum("rskgp,rpkd->rskgd", rounded(weights), cache_values.astype(jnp.float32))
    return summed, highest, total


def local_partial(grouped, fresh_keys, fresh_values, cache_keys, cache_values, lengths):
    grouped_f = grouped.astype(jnp.float32)
    scale = HD ** -0.5
    suffix_scores = jnp.einsum("rskgd,rjkd->rskgj", grouped_f, cache_keys.astype(jnp.float32)) * scale
    fresh_scores = jnp.einsum("rskgd,rtkd->rskgt", grouped_f, fresh_keys.astype(jnp.float32)) * scale
    positions = jnp.arange(cache_keys.shape[1], dtype=jnp.int32)
    suffix_mask = (positions[None, :] < lengths[:, None])[:, None, None, None, :]
    order = jnp.arange(fresh_keys.shape[1], dtype=jnp.int32)
    fresh_mask = (order[None, :] <= order[:, None])[None, :, None, None, :]
    suffix_scores = jnp.where(suffix_mask, suffix_scores, NEGATIVE)
    fresh_scores = jnp.where(fresh_mask, fresh_scores, NEGATIVE)
    highest = jnp.maximum(jnp.max(suffix_scores, axis=-1), jnp.max(fresh_scores, axis=-1))
    suffix_weights = jnp.where(suffix_mask, jnp.exp(suffix_scores - highest[..., None]), 0.0)
    fresh_weights = jnp.where(fresh_mask, jnp.exp(fresh_scores - highest[..., None]), 0.0)
    total = jnp.sum(suffix_weights, axis=-1) + jnp.sum(fresh_weights, axis=-1)
    summed = jnp.einsum("rskgj,rjkd->rskgd", rounded(suffix_weights), cache_values.astype(jnp.float32))
    summed = summed + jnp.einsum("rskgt,rtkd->rskgd", rounded(fresh_weights), fresh_values.astype(jnp.float32))
    return summed, highest, total


def combine(first, second):
    summed_a, highest_a, total_a = first
    summed_b, highest_b, total_b = second
    highest = jnp.maximum(highest_a, highest_b)
    factor_a = jnp.exp(highest_a - highest)
    factor_b = jnp.exp(highest_b - highest)
    summed = summed_a * factor_a[..., None] + summed_b * factor_b[..., None]
    return summed, highest, total_a * factor_a + total_b * factor_b


def reference(queries, new_keys, new_values, suffix_keys, suffix_values, suffix_lengths, prefix_ids, prefix_owner, prefix_keys, prefix_values):
    owner = jnp.take(prefix_owner, prefix_ids[:, 0], axis=0).astype(jnp.int32)
    blocks = queries.shape[0] // R_DEV

    def split_blocks(array):
        return array.reshape((blocks, R_DEV) + array.shape[1:])

    def one_block(items):
        block_queries, block_keys, block_values, block_cache_keys, block_cache_values, block_lengths, block_owner = items
        grouped = block_queries.reshape(R_DEV, STEPS, KVH, GQ, HD)
        first = prefix_partial(grouped, jnp.take(prefix_keys, block_owner, axis=0), jnp.take(prefix_values, block_owner, axis=0))
        second = local_partial(grouped, block_keys, block_values, block_cache_keys, block_cache_values, block_lengths)
        summed, highest, total = combine(first, second)
        return (summed / total[..., None]).reshape(R_DEV, STEPS, QH, HD).astype(jnp.bfloat16)

    arrays = (queries, new_keys, new_values, suffix_keys, suffix_values, suffix_lengths, owner)
    result = lax.map(one_block, tuple(split_blocks(array) for array in arrays))
    return result.reshape(queries.shape)
```

```python
import functools
import math

import jax
import jax.numpy as jnp
from jax import lax
from jax.experimental import pallas as pl
from jax.experimental.pallas import tpu as pltpu
from jax.sharding import PartitionSpec as P

NEGATIVE = -1e30
LOG2E = math.log2(math.e)
MESH = pl.DeviceIdType.MESH
F32 = jnp.float32
BF16 = jnp.bfloat16


def place_kernel(cap, ids_ref, owner_ref, pick_ref, slot_ref, count_ref):
    def clear(i, _):
        pick_ref[i] = 0
        return 0

    lax.fori_loop(0, pick_ref.shape[0], clear, 0)

    def clear_count(i, _):
        count_ref[i] = 0
        return 0

    lax.fori_loop(0, count_ref.shape[0], clear_count, 0)

    def place(r, _):
        owner = owner_ref[ids_ref[r]]
        rank = count_ref[owner]
        count_ref[owner] = rank + 1
        slot = owner * cap + rank
        slot_ref[r] = slot
        pick_ref[slot] = r
        return 0

    lax.fori_loop(0, ids_ref.shape[0], place, 0)


def dot_t(a, b):
    return lax.dot_general(a, b, (((1,), (1,)), ((), ())), preferred_element_type=F32)


def dot(a, b):
    return lax.dot_general(a, b, (((1,), (0,)), ((), ())), preferred_element_type=F32)


def swap_groups(x, outer, inner):
    return jnp.concatenate(
        [x[(o * inner + i) * 8 : (o * inner + i) * 8 + 8] for i in range(inner) for o in range(outer)],
        axis=0,
    )


def kernel(
    n,
    cap,
    kvs,
    steps,
    chunks,
    pick_ref,
    slot_ref,
    len_ref,
    q_hbm,
    nk_ref,
    nv_ref,
    sk_hbm,
    sv_hbm,
    pk_hbm,
    pv_hbm,
    out_ref,
    q_raw,
    q_perm,
    q_send,
    q_recv,
    r_send,
    r_recv,
    t_send,
    t_recv,
    p_raw,
    wide,
    keys,
    values,
    sk,
    sv,
    own_a,
    own_l,
    q_sem,
    p_sem,
    s_sem,
    qs_sem,
    qr_sem,
    rs_sem,
    rr_sem,
    ts_sem,
    tr_sem,
):
    rows, heads, width = q_raw.shape
    per = heads // kvs
    plen = keys.shape[1]
    slots = sk.shape[1]
    scale = width ** (-0.5) * LOG2E
    me = lax.axis_index("dp")

    load_q = pltpu.make_async_copy(q_hbm, q_raw, q_sem)
    load_q.start()
    load_k = pltpu.make_async_copy(pk_hbm, p_raw.at[0], p_sem.at[0])
    load_v = pltpu.make_async_copy(pv_hbm, p_raw.at[1], p_sem.at[1])
    load_k.start()
    load_v.start()
    step = rows // chunks

    def suffix_copies(c):
        part = pl.ds(c * step, step)
        return (
            pltpu.make_async_copy(sk_hbm.at[part], sk.at[part], s_sem.at[0, c]),
            pltpu.make_async_copy(sv_hbm.at[part], sv.at[part], s_sem.at[1, c]),
        )

    barrier = pltpu.get_barrier_semaphore()

    def greet(k, _):
        pl.semaphore_signal(barrier, inc=1, device_id={"dp": lax.rem(me + k, n)}, device_id_type=MESH)
        return 0

    lax.fori_loop(1, n, greet, 0)

    load_q.wait()

    def permute(r, _):
        x = q_raw[r].astype(F32)
        q_perm[r] = swap_groups(x, steps, kvs).astype(BF16)
        return 0

    lax.fori_loop(0, rows, permute, 0)

    def choose(peer, ref):
        def one(j, _):
            s = peer * cap + j
            ref[peer, j] = q_perm[pick_ref[s]]
            return 0

        lax.fori_loop(0, cap, one, 0)

    def q_copy(peer, source):
        return pltpu.make_async_remote_copy(
            src_ref=q_send.at[peer],
            dst_ref=q_recv.at[source],
            send_sem=qs_sem.at[peer],
            recv_sem=qr_sem.at[source],
            device_id={"dp": peer},
            device_id_type=MESH,
        )

    def r_copy(peer, source):
        return pltpu.make_async_remote_copy(
            src_ref=r_send.at[peer],
            dst_ref=r_recv.at[source],
            send_sem=rs_sem.at[peer],
            recv_sem=rr_sem.at[source],
            device_id={"dp": peer},
            device_id_type=MESH,
        )

    def t_copy(peer, source):
        return pltpu.make_async_remote_copy(
            src_ref=t_send.at[peer],
            dst_ref=t_recv.at[source],
            send_sem=ts_sem.at[peer],
            recv_sem=tr_sem.at[source],
            device_id={"dp": peer},
            device_id_type=MESH,
        )

    pl.semaphore_wait(barrier, n - 1)

    def send(k, _):
        peer = lax.rem(me + k, n)
        choose(peer, q_send)
        q_copy(peer, me).start()
        return 0

    lax.fori_loop(1, n, send, 0)
    choose(me, q_recv)

    def start_suffix(c, _):
        for copy in suffix_copies(c):
            copy.start()
        return 0

    lax.fori_loop(0, chunks, start_suffix, 0)

    load_k.wait()
    load_v.wait()
    piece = wide.shape[0] // kvs

    def split(c, _):
        for which in range(2):
            wide[...] = p_raw[which, pl.ds(c * piece * kvs, piece * kvs), :].astype(F32)
            for kv in range(kvs):
                part = wide[pl.ds(kv, piece, stride=kvs), :].astype(BF16)
                if which == 0:
                    keys[kv, pl.ds(c * piece, piece), :] = part
                else:
                    values[kv, pl.ds(c * piece, piece), 0:width] = part
                    values[kv, pl.ds(c * piece, piece), width : 2 * width] = jnp.ones((piece, width), BF16)
        return 0

    lax.fori_loop(0, plen // piece, split, 0)

    group = min(cap, 8)
    lane = lax.broadcasted_iota(jnp.int32, (per, width), 1)
    line = lax.broadcasted_iota(jnp.int32, (per, width), 0)

    def attend(source):
        def part(c, _):
            where = pl.ds(c * group, group)
            stat = jnp.zeros((group, width), F32)
            for kv in range(kvs):
                q = q_recv[source, where, kv * per : (kv + 1) * per, :].reshape(group * per, width)
                s = dot_t(q, keys[kv])
                top = jnp.max(s, axis=-1, keepdims=True) * scale
                w = jnp.exp2(s * scale - top).astype(BF16)
                both = dot(w, values[kv])
                total = both[:, width : 2 * width]
                a = both[:, 0:width] / total
                r_send[source, where, kv * per : (kv + 1) * per, :] = a.astype(BF16).reshape(group, per, width)
                level = (top + jnp.log(total) * LOG2E).reshape(group, per, width)
                stat = stat + jnp.sum(jnp.where((lane == line + kv * per)[None], level, 0.0), axis=1)
            t_send[source, where, :, :] = stat.reshape(group, 1, width)
            return 0

        lax.fori_loop(0, cap // group, part, 0)

    attend(me)

    fresh = nk_ref.shape[0] // rows
    row = lax.broadcasted_iota(jnp.int32, (heads, slots), 0)
    col = lax.broadcasted_iota(jnp.int32, (heads, slots), 1)
    same = lax.rem(col, kvs) == row // per
    position = jnp.where(same, col // kvs, slots)
    nrow = lax.broadcasted_iota(jnp.int32, (2 * heads, 2 * fresh), 0)
    ncol = lax.broadcasted_iota(jnp.int32, (2 * heads, 2 * fresh), 1)
    nrow_in, ncol_in = lax.rem(nrow, heads), lax.rem(ncol, fresh)
    fresh_mask = (
        (nrow // heads == ncol // fresh)
        & (nrow_in // per == lax.rem(ncol_in, kvs))
        & (ncol_in // kvs <= lax.rem(nrow_in, per) // (per // steps))
    )

    def local(pair):
        first = pair * 2
        q2 = q_perm[pl.ds(first, 2)].reshape(2 * heads, width)
        new = pl.ds(pl.multiple_of(pair * 2 * fresh, 2 * fresh), 2 * fresh)
        sn = jnp.where(fresh_mask, dot_t(q2, nk_ref[new, :]), NEGATIVE)
        top_n = jnp.max(sn, axis=-1, keepdims=True)
        scores, tops = [], []
        for i in range(2):
            s = dot_t(q2[i * heads : (i + 1) * heads], sk[first + i])
            s = jnp.where(position < len_ref[first + i], s, NEGATIVE)
            scores.append(s)
            tops.append(jnp.maximum(jnp.max(s, axis=-1, keepdims=True), top_n[i * heads : (i + 1) * heads]))
        top = jnp.concatenate(tops, axis=0)
        wn = jnp.exp2((sn - top) * scale)
        total_n = jnp.sum(wn, axis=-1, keepdims=True)
        un = dot(wn.astype(BF16), nv_ref[new, :])
        for i in range(2):
            half = slice(i * heads, (i + 1) * heads)
            w = jnp.exp2((scores[i] - tops[i]) * scale)
            total = jnp.sum(w, axis=-1, keepdims=True) + total_n[half]
            u = dot(w.astype(BF16), sv[first + i]) + un[half]
            own_a[first + i] = u / total
            own_l[first + i] = tops[i] * scale + jnp.log(total) * LOG2E

    def local_chunk(c, _):
        for copy in suffix_copies(c):
            copy.wait()

        def one(i, _):
            local(c * (step // 2) + i)
            return 0

        lax.fori_loop(0, step // 2, one, 0)
        return 0

    lax.fori_loop(0, chunks, local_chunk, 0)

    def serve(k, _):
        source = lax.rem(me + n - k, n)
        q_copy(source, source).wait_recv()
        attend(source)
        r_copy(source, me).start()
        t_copy(source, me).start()
        return 0

    lax.fori_loop(1, n, serve, 0)

    r_recv[me] = r_send[me]
    t_recv[me] = t_send[me]

    def finish(k, _):
        peer = lax.rem(me + k, n)
        r_copy(peer, peer).wait_recv()
        t_copy(peer, peer).wait_recv()
        return 0

    lax.fori_loop(1, n, finish, 0)

    lane_h = lax.broadcasted_iota(jnp.int32, (heads, width), 1)
    line_h = lax.broadcasted_iota(jnp.int32, (heads, width), 0)

    def merge(r, _):
        place = slot_ref[r]
        a1 = r_recv[place // cap, lax.rem(place, cap)].astype(F32)
        stat = t_recv[place // cap, lax.rem(place, cap)]
        level = jnp.sum(jnp.where(lane_h == line_h, stat, 0.0), axis=1, keepdims=True)
        share = 1.0 / (1.0 + jnp.exp2(own_l[r] - level))
        a2 = own_a[r]
        out = a2 + (a1 - a2) * share
        out_ref[r] = swap_groups(out, kvs, steps).astype(BF16)
        return 0

    lax.fori_loop(0, rows, merge, 0)

    def drain(k, _):
        peer = lax.rem(me + k, n)
        q_copy(peer, me).wait_send()
        r_copy(peer, me).wait_send()
        t_copy(peer, me).wait_send()
        return 0

    lax.fori_loop(1, n, drain, 0)


def on_device(
    n,
    queries,
    new_keys,
    new_values,
    suffix_keys,
    suffix_values,
    suffix_lengths,
    prefix_ids,
    prefix_owner,
    prefix_keys,
    prefix_values,
):
    rows, steps, head_count, width = queries.shape
    kvs = new_keys.shape[2]
    heads = steps * head_count
    slen = suffix_keys.shape[1]
    plen = prefix_keys.shape[1]
    cap = max(2, 2 * rows // n)
    chunks = 8
    smem = pl.BlockSpec(memory_space=pltpu.SMEM)
    vmem = pl.BlockSpec(memory_space=pltpu.VMEM)
    hbm = pl.BlockSpec(memory_space=pl.ANY)

    pick, slot = pl.pallas_call(
        functools.partial(place_kernel, cap),
        out_shape=(
            jax.ShapeDtypeStruct((n * cap,), jnp.int32),
            jax.ShapeDtypeStruct((rows,), jnp.int32),
        ),
        in_specs=[smem, smem],
        out_specs=(smem, smem),
        scratch_shapes=[pltpu.SMEM((n,), jnp.int32)],
    )(prefix_ids.reshape(rows), prefix_owner)

    flops = 4 * n * cap * heads * plen * width + 4 * rows * heads * kvs * slen * width
    out = pl.pallas_call(
        functools.partial(kernel, n, cap, kvs, steps, chunks),
        out_shape=jax.ShapeDtypeStruct((rows, heads, width), BF16),
        in_specs=[smem, smem, smem, hbm, vmem, vmem, hbm, hbm, hbm, hbm],
        out_specs=vmem,
        scratch_shapes=[
            pltpu.VMEM((rows, heads, width), BF16),
            pltpu.VMEM((rows, heads, width), BF16),
            pltpu.VMEM((n, cap, heads, width), BF16),
            pltpu.VMEM((n, cap, heads, width), BF16),
            pltpu.VMEM((n, cap, heads, width), BF16),
            pltpu.VMEM((n, cap, heads, width), BF16),
            pltpu.VMEM((n, cap, 1, width), F32),
            pltpu.VMEM((n, cap, 1, width), F32),
            pltpu.VMEM((2, plen * kvs, width), BF16),
            pltpu.VMEM((256 * kvs, width), F32),
            pltpu.VMEM((kvs, plen, width), BF16),
            pltpu.VMEM((kvs, plen, 2 * width), BF16),
            pltpu.VMEM((rows, slen * kvs, width), BF16),
            pltpu.VMEM((rows, slen * kvs, width), BF16),
            pltpu.VMEM((rows, heads, width), F32),
            pltpu.VMEM((rows, heads, 1), F32),
            pltpu.SemaphoreType.DMA,
            pltpu.SemaphoreType.DMA((2,)),
            pltpu.SemaphoreType.DMA((2, chunks)),
            pltpu.SemaphoreType.DMA((n,)),
            pltpu.SemaphoreType.DMA((n,)),
            pltpu.SemaphoreType.DMA((n,)),
            pltpu.SemaphoreType.DMA((n,)),
            pltpu.SemaphoreType.DMA((n,)),
            pltpu.SemaphoreType.DMA((n,)),
        ],
        compiler_params=pltpu.CompilerParams(
            collective_id=0, has_side_effects=True, vmem_limit_bytes=58 * 1024 * 1024
        ),
        cost_estimate=pl.CostEstimate(
            flops=flops, bytes_accessed=24 * 1024 * 1024, transcendentals=n * cap * heads * plen
        ),
    )(
        pick,
        slot,
        suffix_lengths,
        queries.reshape(rows, heads, width),
        new_keys.reshape(rows * steps * kvs, width),
        new_values.reshape(rows * steps * kvs, width),
        suffix_keys.reshape(rows, slen * kvs, width),
        suffix_values.reshape(rows, slen * kvs, width),
        prefix_keys.reshape(plen * kvs, width),
        prefix_values.reshape(plen * kvs, width),
    )
    return out.reshape(queries.shape)


def solution(mesh):
    in_specs = (
        P("dp", None, "tp", None),
        P("dp", None, "tp", None),
        P("dp", None, "tp", None),
        P("dp", None, "tp", None),
        P("dp", None, "tp", None),
        P("dp"),
        P("dp", None),
        P(),
        P("dp", None, "tp", None),
        P("dp", None, "tp", None),
    )
    out_specs = P("dp", None, "tp", None)
    return jax.shard_map(
        functools.partial(on_device, mesh.shape["dp"]),
        mesh=mesh,
        in_specs=in_specs,
        out_specs=out_specs,
        check_vma=False,
    )
```

```python
import functools
import math

import jax
import jax.numpy as jnp
from jax import lax
from jax.experimental import pallas as pl
from jax.experimental.pallas import tpu as pltpu
from jax.sharding import PartitionSpec as P

NEGATIVE = -1e30
LOG2E = math.log2(math.e)
MESH = pl.DeviceIdType.MESH
F32 = jnp.float32
BF16 = jnp.bfloat16


def place(ids, owner_ref, cap, table):
    rows, lanes = ids.shape[1], table.shape[1]
    owner = jnp.zeros((1, rows), jnp.int32)
    for p in range(owner_ref.shape[0]):
        owner = owner + jnp.where(ids == p, owner_ref[p], 0)
    down = lax.broadcasted_iota(jnp.int32, (rows, rows), 0)
    across = lax.broadcasted_iota(jnp.int32, (rows, rows), 1)

    def column(row):
        return jnp.sum(jnp.where(down == across, row, 0), axis=1, keepdims=True)

    earlier = (column(owner) == owner) & (down < across)
    slot = owner * cap + jnp.sum(jnp.where(earlier, 1, 0), axis=0, keepdims=True)
    here = column(slot) == lax.broadcasted_iota(jnp.int32, (rows, lanes), 1)
    request = lax.broadcasted_iota(jnp.int32, (rows, lanes), 0)
    table[...] = jnp.zeros_like(table)
    table[0:1, 0:rows] = slot
    table[1:2, :] = jnp.sum(jnp.where(here, request, 0), axis=0, keepdims=True)


def dot_t(a, b):
    return lax.dot_general(a, b, (((1,), (1,)), ((), ())), preferred_element_type=F32)


def dot(a, b):
    return lax.dot_general(a, b, (((1,), (0,)), ((), ())), preferred_element_type=F32)


def partner(me, k, n):
    if n & (n - 1):
        return lax.rem(me + k, n)
    total, bit = 0, 1
    while bit < n:
        mine, other = lax.rem(me // bit, 2), lax.rem(k // bit, 2)
        total = total + bit * (mine + other - 2 * mine * other)
        bit *= 2
    return total


def source_of(me, k, n):
    return lax.rem(me + n - k, n) if n & (n - 1) else partner(me, k, n)


def turn(i, n):
    if n % 2:
        return i
    half = n // 2 - 1
    return jnp.where(i == 1, 1, (lax.rem(i - 2, half) + 1) * 2 + (i - 2) // half)


def kernel(
    n,
    cap,
    kvs,
    steps,
    fresh,
    chunks,
    ids_ref,
    owner_ref,
    len_ref,
    q_hbm,
    nk_hbm,
    nv_hbm,
    sk_hbm,
    sv_hbm,
    pk_hbm,
    pv_hbm,
    out_hbm,
    table,
    places,
    nk_ref,
    nv_ref,
    out_ref,
    level_ref,
    q_raw,
    q_send,
    q_recv,
    r_send,
    r_recv,
    t_send,
    t_recv,
    p_raw,
    wide,
    keys,
    values,
    sk,
    sv,
    own_a,
    own_l,
    table_sem,
    n_sem,
    o_sem,
    q_sem,
    p_sem,
    s_sem,
    qs_sem,
    qr_sem,
    rs_sem,
    rr_sem,
    ts_sem,
    tr_sem,
):
    rows, heads, width = q_raw.shape
    per = heads // kvs
    plen = keys.shape[1]
    slots = sk.shape[1]
    scale = width ** (-0.5) * LOG2E
    me = lax.axis_index("dp")

    load_q = pltpu.make_async_copy(q_hbm, q_raw, q_sem)
    load_q.start()
    load_k = pltpu.make_async_copy(pk_hbm, p_raw.at[0], p_sem.at[0])
    load_v = pltpu.make_async_copy(pv_hbm, p_raw.at[1], p_sem.at[1])
    load_k.start()
    load_v.start()
    load_nk = pltpu.make_async_copy(nk_hbm, nk_ref, n_sem.at[0])
    load_nv = pltpu.make_async_copy(nv_hbm, nv_ref, n_sem.at[1])
    load_nk.start()
    load_nv.start()
    step = rows // chunks

    def suffix_copies(c):
        part = pl.ds(c * step, step)
        return (
            pltpu.make_async_copy(sk_hbm.at[part], sk.at[part], s_sem.at[0, c]),
            pltpu.make_async_copy(sv_hbm.at[part], sv.at[part], s_sem.at[1, c]),
        )

    barrier = pltpu.get_barrier_semaphore()

    def greet(k, _):
        pl.semaphore_signal(barrier, inc=1, device_id={"dp": lax.rem(me + k, n)}, device_id_type=MESH)
        return 0

    lax.fori_loop(1, n, greet, 0)

    place(ids_ref[...], owner_ref, cap, table)
    put = pltpu.make_async_copy(table, places, table_sem)
    put.start()
    put.wait()
    load_q.wait()

    def choose(peer, ref):
        def one(j, _):
            s = peer * cap + j
            ref[peer, j] = q_raw[places[1, s]]
            return 0

        lax.fori_loop(0, cap, one, 0)

    def q_copy(peer, source):
        return pltpu.make_async_remote_copy(
            src_ref=q_send.at[peer],
            dst_ref=q_recv.at[source],
            send_sem=qs_sem.at[peer],
            recv_sem=qr_sem.at[source],
            device_id={"dp": peer},
            device_id_type=MESH,
        )

    def r_copy(peer, source):
        return pltpu.make_async_remote_copy(
            src_ref=r_send.at[peer],
            dst_ref=r_recv.at[source],
            send_sem=rs_sem.at[peer],
            recv_sem=rr_sem.at[source],
            device_id={"dp": peer},
            device_id_type=MESH,
        )

    def t_copy(peer, source):
        return pltpu.make_async_remote_copy(
            src_ref=t_send.at[peer],
            dst_ref=t_recv.at[source],
            send_sem=ts_sem.at[peer],
            recv_sem=tr_sem.at[source],
            device_id={"dp": peer},
            device_id_type=MESH,
        )

    pl.semaphore_wait(barrier, n - 1)

    def send(i, _):
        peer = partner(me, turn(i, n), n)
        choose(peer, q_send)
        q_copy(peer, me).start()
        return 0

    lax.fori_loop(1, n, send, 0)
    choose(me, q_recv)

    def start_suffix(c, _):
        for copy in suffix_copies(c):
            copy.start()
        return 0

    lax.fori_loop(0, chunks, start_suffix, 0)

    load_k.wait()
    load_v.wait()
    piece = wide.shape[0] // kvs

    def split(c, _):
        for which in range(2):
            wide[...] = p_raw[which, pl.ds(c * piece * kvs, piece * kvs), :].astype(F32)
            for kv in range(kvs):
                part = wide[pl.ds(kv, piece, stride=kvs), :].astype(BF16)
                if which == 0:
                    keys[kv, pl.ds(c * piece, piece), :] = part
                else:
                    values[kv, pl.ds(c * piece, piece), 0:width] = part
                    values[kv, pl.ds(c * piece, piece), width : 2 * width] = jnp.ones((piece, width), BF16)
        return 0

    lax.fori_loop(0, plen // piece, split, 0)

    gq = per // steps
    lane = lax.broadcasted_iota(jnp.int32, (per, width), 1)
    line = lax.broadcasted_iota(jnp.int32, (per, width), 0)
    natural = (line // gq) * (gq * kvs) + lax.rem(line, gq)

    def attend(source):
        grouped = q_recv[source].astype(F32).reshape(cap * steps, kvs, gq, width)
        scores = [
            dot_t(grouped[:, kv].reshape(cap * per, width).astype(BF16), keys[kv]) for kv in range(kvs)
        ]
        stat = jnp.zeros((cap, width), F32)
        parts = []
        for kv in range(kvs):
            s = scores[kv]
            top = jnp.max(s, axis=-1, keepdims=True) * scale
            w = jnp.exp2(s * scale - top).astype(BF16)
            both = dot(w, values[kv])
            total = both[:, width : 2 * width]
            parts.append((both[:, 0:width] / total).reshape(cap * steps, 1, gq, width))
            level = (top + jnp.log(total) * LOG2E).reshape(cap, per, width)
            stat = stat + jnp.sum(jnp.where((lane == natural + kv * gq)[None], level, 0.0), axis=1)
        joined = jnp.concatenate(parts, axis=1) if kvs > 1 else parts[0]
        r_send[source] = joined.reshape(cap, heads, width).astype(BF16)
        t_send[source] = stat.reshape(cap, 1, width)

    early = chunks // 2

    attend(me)

    row = lax.broadcasted_iota(jnp.int32, (heads, slots), 0)
    col = lax.broadcasted_iota(jnp.int32, (heads, slots), 1)
    same = lax.rem(col, kvs) == lax.rem(row // gq, kvs)
    position = jnp.where(same, col // kvs, slots)
    many = 4
    nrow = lax.broadcasted_iota(jnp.int32, (many * heads, many * fresh), 0)
    ncol = lax.broadcasted_iota(jnp.int32, (many * heads, many * fresh), 1)
    nrow_in, ncol_in = lax.rem(nrow, heads), lax.rem(ncol, fresh)
    fresh_mask = (
        (nrow // heads == ncol // fresh)
        & (lax.rem(nrow_in // gq, kvs) == lax.rem(ncol_in, kvs))
        & (ncol_in // kvs <= nrow_in // (gq * kvs))
    )

    def local(index):
        first = index * many
        q = q_raw[pl.ds(first, many)].reshape(many * heads, width)
        new = pl.ds(pl.multiple_of(index * many * fresh, many * fresh), many * fresh)
        half = [slice(i * heads, (i + 1) * heads) for i in range(many)]
        scores = [dot_t(q[half[i]], sk[first + i]) for i in range(many)]
        sn = jnp.where(fresh_mask, dot_t(q, nk_ref[new, :]), NEGATIVE)
        top_n = jnp.max(sn, axis=-1, keepdims=True)
        scores = [jnp.where(position < len_ref[first + i], scores[i], NEGATIVE) for i in range(many)]
        tops = [
            jnp.maximum(jnp.max(scores[i], axis=-1, keepdims=True), top_n[half[i]]) for i in range(many)
        ]
        wn = jnp.exp2((sn - jnp.concatenate(tops, axis=0)) * scale)
        total_n = jnp.sum(wn, axis=-1, keepdims=True)
        un = dot(wn.astype(BF16), nv_ref[new, :])
        weights = [jnp.exp2((scores[i] - tops[i]) * scale) for i in range(many)]
        summed = [dot(weights[i].astype(BF16), sv[first + i]) for i in range(many)]
        for i in range(many):
            total = jnp.sum(weights[i], axis=-1, keepdims=True) + total_n[half[i]]
            own_a[first + i] = (summed[i] + un[half[i]]) / total
            own_l[first + i] = jnp.broadcast_to(tops[i] * scale + jnp.log(total) * LOG2E, (heads, width))

    load_nk.wait()
    load_nv.wait()

    def local_chunk(c, _):
        for copy in suffix_copies(c):
            copy.wait()

        def one(i, _):
            local(c * (step // many) + i)
            return 0

        lax.fori_loop(0, step // many, one, 0)
        return 0

    lax.fori_loop(0, early, local_chunk, 0)

    def serve(i, _):
        source = source_of(me, turn(i, n), n)
        q_copy(source, source).wait_recv()
        attend(source)
        r_copy(source, me).start()
        t_copy(source, me).start()
        return 0

    lax.fori_loop(1, n, serve, 0)
    lax.fori_loop(early, chunks, local_chunk, 0)

    r_recv[me] = r_send[me]
    t_recv[me] = t_send[me]

    spread = lax.broadcasted_iota(jnp.int32, (cap, heads, width), 2) == lax.broadcasted_iota(
        jnp.int32, (cap, heads, width), 1
    )

    def widen(owner):
        level = jnp.sum(jnp.where(spread, t_recv[owner], 0.0), axis=2, keepdims=True)
        level_ref[owner] = jnp.broadcast_to(level, (cap, heads, width))

    widen(me)

    def finish(i, _):
        peer = partner(me, turn(i, n), n)
        t_copy(peer, peer).wait_recv()
        widen(peer)
        r_copy(peer, peer).wait_recv()
        return 0

    lax.fori_loop(1, n, finish, 0)

    def out_copy(c):
        part = pl.ds(c * step, step)
        return pltpu.make_async_copy(out_ref.at[part], out_hbm.at[part], o_sem.at[c])

    def merge_chunk(c, _):
        def merge(index, _):
            first = c * step + index * many
            results = []
            for i in range(many):
                slot = places[0, first + i]
                owner, rank = slot // cap, lax.rem(slot, cap)
                a1 = r_recv[owner, rank].astype(F32)
                share = 1.0 / (1.0 + jnp.exp2(own_l[first + i] - level_ref[owner, rank]))
                a2 = own_a[first + i]
                results.append((a2 + (a1 - a2) * share).astype(BF16))
            for i in range(many):
                out_ref[first + i] = results[i]
            return 0

        lax.fori_loop(0, step // many, merge, 0)
        out_copy(c).start()
        return 0

    lax.fori_loop(0, chunks, merge_chunk, 0)

    def drain_out(c, _):
        out_copy(c).wait()
        return 0

    lax.fori_loop(0, chunks, drain_out, 0)

    def drain(k, _):
        peer = lax.rem(me + k, n)
        q_copy(peer, me).wait_send()
        r_copy(peer, me).wait_send()
        t_copy(peer, me).wait_send()
        return 0

    lax.fori_loop(1, n, drain, 0)


def on_device(
    n,
    queries,
    new_keys,
    new_values,
    suffix_keys,
    suffix_values,
    suffix_lengths,
    prefix_ids,
    prefix_owner,
    prefix_keys,
    prefix_values,
):
    rows, steps, head_count, width = queries.shape
    kvs = new_keys.shape[2]
    heads = steps * head_count
    slen = suffix_keys.shape[1]
    plen = prefix_keys.shape[1]
    cap = max(2, 2 * rows // n)
    chunks = 4
    smem = pl.BlockSpec(memory_space=pltpu.SMEM)
    vmem = pl.BlockSpec(memory_space=pltpu.VMEM)
    hbm = pl.BlockSpec(memory_space=pl.ANY)

    flops = 4 * n * cap * heads * plen * width + 4 * rows * heads * kvs * slen * width
    out = pl.pallas_call(
        functools.partial(kernel, n, cap, kvs, steps, steps * kvs, chunks),
        out_shape=jax.ShapeDtypeStruct((rows, heads, width), BF16),
        in_specs=[vmem, smem, smem, hbm, hbm, hbm, hbm, hbm, hbm, hbm],
        out_specs=hbm,
        scratch_shapes=[
            pltpu.VMEM((2, n * cap), jnp.int32),
            pltpu.SMEM((2, n * cap), jnp.int32),
            pltpu.VMEM((rows * steps * kvs, width), BF16),
            pltpu.VMEM((rows * steps * kvs, width), BF16),
            pltpu.VMEM((rows, heads, width), BF16),
            pltpu.VMEM((n, cap, heads, width), F32),
            pltpu.VMEM((rows, heads, width), BF16),
            pltpu.VMEM((n, cap, heads, width), BF16),
            pltpu.VMEM((n, cap, heads, width), BF16),
            pltpu.VMEM((n, cap, heads, width), BF16),
            pltpu.VMEM((n, cap, heads, width), BF16),
            pltpu.VMEM((n, cap, 1, width), F32),
            pltpu.VMEM((n, cap, 1, width), F32),
            pltpu.VMEM((2, plen * kvs, width), BF16),
            pltpu.VMEM((256 * kvs, width), F32),
            pltpu.VMEM((kvs, plen, width), BF16),
            pltpu.VMEM((kvs, plen, 2 * width), BF16),
            pltpu.VMEM((rows, slen * kvs, width), BF16),
            pltpu.VMEM((rows, slen * kvs, width), BF16),
            pltpu.VMEM((rows, heads, width), F32),
            pltpu.VMEM((rows, heads, width), F32),
            pltpu.SemaphoreType.DMA,
            pltpu.SemaphoreType.DMA((2,)),
            pltpu.SemaphoreType.DMA((chunks,)),
            pltpu.SemaphoreType.DMA,
            pltpu.SemaphoreType.DMA((2,)),
            pltpu.SemaphoreType.DMA((2, chunks)),
            pltpu.SemaphoreType.DMA((n,)),
            pltpu.SemaphoreType.DMA((n,)),
            pltpu.SemaphoreType.DMA((n,)),
            pltpu.SemaphoreType.DMA((n,)),
            pltpu.SemaphoreType.DMA((n,)),
            pltpu.SemaphoreType.DMA((n,)),
        ],
        compiler_params=pltpu.CompilerParams(
            collective_id=0, has_side_effects=True, vmem_limit_bytes=58 * 1024 * 1024
        ),
        cost_estimate=pl.CostEstimate(
            flops=flops, bytes_accessed=24 * 1024 * 1024, transcendentals=n * cap * heads * plen
        ),
    )(
        prefix_ids.reshape(1, rows),
        prefix_owner,
        suffix_lengths,
        queries.reshape(rows, heads, width),
        new_keys.reshape(rows * steps * kvs, width),
        new_values.reshape(rows * steps * kvs, width),
        suffix_keys.reshape(rows, slen * kvs, width),
        suffix_values.reshape(rows, slen * kvs, width),
        prefix_keys.reshape(plen * kvs, width),
        prefix_values.reshape(plen * kvs, width),
    )
    return out.reshape(queries.shape)


def solution(mesh):
    in_specs = (
        P("dp", None, "tp", None),
        P("dp", None, "tp", None),
        P("dp", None, "tp", None),
        P("dp", None, "tp", None),
        P("dp", None, "tp", None),
        P("dp"),
        P("dp", None),
        P(),
        P("dp", None, "tp", None),
        P("dp", None, "tp", None),
    )
    out_specs = P("dp", None, "tp", None)
    return jax.shard_map(
        functools.partial(on_device, mesh.shape["dp"]),
        mesh=mesh,
        in_specs=in_specs,
        out_specs=out_specs,
        check_vma=False,
    )
```

```python
import functools
import math

import jax
import jax.numpy as jnp
from jax import lax
from jax.experimental import pallas as pl
from jax.experimental.pallas import tpu as pltpu
from jax.sharding import PartitionSpec as P

NEGATIVE = -1e30
LOG2E = math.log2(math.e)
MESH = pl.DeviceIdType.MESH
F32 = jnp.float32
BF16 = jnp.bfloat16


def place(ids, owner_ref, cap, table):
    rows, lanes = ids.shape[1], table.shape[1]
    owner = jnp.zeros((1, rows), jnp.int32)
    for p in range(owner_ref.shape[0]):
        owner = owner + jnp.where(ids == p, owner_ref[p], 0)
    down = lax.broadcasted_iota(jnp.int32, (rows, rows), 0)
    across = lax.broadcasted_iota(jnp.int32, (rows, rows), 1)

    def column(row):
        return jnp.sum(jnp.where(down == across, row, 0), axis=1, keepdims=True)

    earlier = (column(owner) == owner) & (down < across)
    slot = owner * cap + jnp.sum(jnp.where(earlier, 1, 0), axis=0, keepdims=True)
    here = column(slot) == lax.broadcasted_iota(jnp.int32, (rows, lanes), 1)
    request = lax.broadcasted_iota(jnp.int32, (rows, lanes), 0)
    table[...] = jnp.zeros_like(table)
    table[0:1, 0:rows] = slot
    table[1:2, :] = jnp.sum(jnp.where(here, request, 0), axis=0, keepdims=True)


def dot_t(a, b):
    return lax.dot_general(a, b, (((1,), (1,)), ((), ())), preferred_element_type=F32)


def dot(a, b):
    return lax.dot_general(a, b, (((1,), (0,)), ((), ())), preferred_element_type=F32)


def partner(me, k, n):
    if n & (n - 1):
        return lax.rem(me + k, n)
    total, bit = 0, 1
    while bit < n:
        mine, other = lax.rem(me // bit, 2), lax.rem(k // bit, 2)
        total = total + bit * (mine + other - 2 * mine * other)
        bit *= 2
    return total


def source_of(me, k, n):
    return lax.rem(me + n - k, n) if n & (n - 1) else partner(me, k, n)


def turn(i, n):
    if n % 2:
        return i
    half = n // 2 - 1
    return jnp.where(i == 1, 1, (half - lax.rem(i - 2, half)) * 2 + (i - 2) // half)


def kernel(
    n,
    cap,
    kvs,
    steps,
    fresh,
    chunks,
    ids_ref,
    owner_ref,
    len_ref,
    q_hbm,
    nk_hbm,
    nv_hbm,
    sk_hbm,
    sv_hbm,
    pk_hbm,
    pv_hbm,
    out_hbm,
    table,
    places,
    nk_ref,
    nv_ref,
    out_ref,
    level_ref,
    q_raw,
    q_send,
    q_recv,
    r_send,
    r_recv,
    t_send,
    t_recv,
    p_raw,
    wide,
    keys,
    values,
    sk,
    sv,
    own_a,
    own_l,
    table_sem,
    n_sem,
    o_sem,
    q_sem,
    p_sem,
    s_sem,
    qs_sem,
    qr_sem,
    rs_sem,
    rr_sem,
    ts_sem,
    tr_sem,
):
    rows, heads, width = q_raw.shape
    per = heads // kvs
    plen = keys.shape[1]
    slots = sk.shape[1]
    scale = width ** (-0.5) * LOG2E
    me = lax.axis_index("dp")

    load_q = pltpu.make_async_copy(q_hbm, q_raw, q_sem)
    load_q.start()
    load_k = pltpu.make_async_copy(pk_hbm, p_raw.at[0], p_sem.at[0])
    load_v = pltpu.make_async_copy(pv_hbm, p_raw.at[1], p_sem.at[1])
    load_k.start()
    load_v.start()
    load_nk = pltpu.make_async_copy(nk_hbm, nk_ref, n_sem.at[0])
    load_nv = pltpu.make_async_copy(nv_hbm, nv_ref, n_sem.at[1])
    load_nk.start()
    load_nv.start()
    step = rows // chunks

    def suffix_copies(c):
        part = pl.ds(c * step, step)
        return (
            pltpu.make_async_copy(sk_hbm.at[part], sk.at[part], s_sem.at[0, c]),
            pltpu.make_async_copy(sv_hbm.at[part], sv.at[part], s_sem.at[1, c]),
        )

    barrier = pltpu.get_barrier_semaphore()

    def greet(k, _):
        pl.semaphore_signal(barrier, inc=1, device_id={"dp": lax.rem(me + k, n)}, device_id_type=MESH)
        return 0

    lax.fori_loop(1, n, greet, 0)

    place(ids_ref[...], owner_ref, cap, table)
    put = pltpu.make_async_copy(table, places, table_sem)
    put.start()
    put.wait()
    load_q.wait()

    def choose(peer, ref):
        def one(j, _):
            s = peer * cap + j
            ref[peer, j] = q_raw[places[1, s]]
            return 0

        lax.fori_loop(0, cap, one, 0)

    def q_copy(peer, source):
        return pltpu.make_async_remote_copy(
            src_ref=q_send.at[peer],
            dst_ref=q_recv.at[source],
            send_sem=qs_sem.at[peer],
            recv_sem=qr_sem.at[source],
            device_id={"dp": peer},
            device_id_type=MESH,
        )

    def r_copy(peer, source):
        return pltpu.make_async_remote_copy(
            src_ref=r_send.at[peer],
            dst_ref=r_recv.at[source],
            send_sem=rs_sem.at[peer],
            recv_sem=rr_sem.at[source],
            device_id={"dp": peer},
            device_id_type=MESH,
        )

    def t_copy(peer, source):
        return pltpu.make_async_remote_copy(
            src_ref=t_send.at[peer],
            dst_ref=t_recv.at[source],
            send_sem=ts_sem.at[peer],
            recv_sem=tr_sem.at[source],
            device_id={"dp": peer},
            device_id_type=MESH,
        )

    pl.semaphore_wait(barrier, n - 1)

    def send(i, _):
        peer = partner(me, turn(i, n), n)
        choose(peer, q_send)
        q_copy(peer, me).start()
        return 0

    lax.fori_loop(1, n, send, 0)
    choose(me, q_recv)

    def start_suffix(c, _):
        for copy in suffix_copies(c):
            copy.start()
        return 0

    lax.fori_loop(0, chunks, start_suffix, 0)

    load_k.wait()
    load_v.wait()
    piece = wide.shape[0] // kvs

    def split(c, _):
        for which in range(2):
            wide[...] = p_raw[which, pl.ds(c * piece * kvs, piece * kvs), :].astype(F32)
            for kv in range(kvs):
                part = wide[pl.ds(kv, piece, stride=kvs), :].astype(BF16)
                if which == 0:
                    keys[kv, pl.ds(c * piece, piece), :] = part
                else:
                    values[kv, pl.ds(c * piece, piece), 0:width] = part
                    values[kv, pl.ds(c * piece, piece), width : 2 * width] = jnp.ones((piece, width), BF16)
        return 0

    lax.fori_loop(0, plen // piece, split, 0)

    gq = per // steps
    lane = lax.broadcasted_iota(jnp.int32, (per, width), 1)
    line = lax.broadcasted_iota(jnp.int32, (per, width), 0)
    natural = (line // gq) * (gq * kvs) + lax.rem(line, gq)
    fold = cap // t_send.shape[1]
    offset = lax.rem(lax.broadcasted_iota(jnp.int32, (cap, per, width), 0), fold) * heads

    def attend(source):
        grouped = q_recv[source].astype(F32).reshape(cap * steps, kvs, gq, width)
        scores = [
            dot_t(grouped[:, kv].reshape(cap * per, width).astype(BF16), keys[kv]) for kv in range(kvs)
        ]
        stat = jnp.zeros((cap, width), F32)
        parts = []
        for kv in range(kvs):
            s = scores[kv]
            top = jnp.max(s, axis=-1, keepdims=True) * scale
            w = jnp.exp2(s * scale - top).astype(BF16)
            both = dot(w, values[kv])
            total = both[:, width : 2 * width]
            parts.append((both[:, 0:width] / total).reshape(cap * steps, 1, gq, width))
            level = (top + jnp.log(total) * LOG2E).reshape(cap, per, width)
            stat = stat + jnp.sum(jnp.where(offset == (lane - natural - kv * gq)[None], level, 0.0), axis=1)
        joined = jnp.concatenate(parts, axis=1) if kvs > 1 else parts[0]
        r_send[source] = joined.reshape(cap, heads, width).astype(BF16)
        t_send[source] = jnp.sum(stat.reshape(cap // fold, fold, width), axis=1, keepdims=True)

    early = chunks // 2

    attend(me)

    row = lax.broadcasted_iota(jnp.int32, (heads, slots), 0)
    col = lax.broadcasted_iota(jnp.int32, (heads, slots), 1)
    same = lax.rem(col, kvs) == lax.rem(row // gq, kvs)
    position = jnp.where(same, col // kvs, slots)
    many = 4
    nrow = lax.broadcasted_iota(jnp.int32, (many * heads, many * fresh), 0)
    ncol = lax.broadcasted_iota(jnp.int32, (many * heads, many * fresh), 1)
    nrow_in, ncol_in = lax.rem(nrow, heads), lax.rem(ncol, fresh)
    fresh_mask = (
        (nrow // heads == ncol // fresh)
        & (lax.rem(nrow_in // gq, kvs) == lax.rem(ncol_in, kvs))
        & (ncol_in // kvs <= nrow_in // (gq * kvs))
    )

    def local(index):
        first = index * many
        q = q_raw[pl.ds(first, many)].reshape(many * heads, width)
        new = pl.ds(pl.multiple_of(index * many * fresh, many * fresh), many * fresh)
        half = [slice(i * heads, (i + 1) * heads) for i in range(many)]
        scores = [dot_t(q[half[i]], sk[first + i]) for i in range(many)]
        sn = jnp.where(fresh_mask, dot_t(q, nk_ref[new, :]), NEGATIVE)
        top_n = jnp.max(sn, axis=-1, keepdims=True)
        scores = [jnp.where(position < len_ref[first + i], scores[i], NEGATIVE) for i in range(many)]
        tops = [
            jnp.maximum(jnp.max(scores[i], axis=-1, keepdims=True), top_n[half[i]]) for i in range(many)
        ]
        wn = jnp.exp2((sn - jnp.concatenate(tops, axis=0)) * scale)
        total_n = jnp.sum(wn, axis=-1, keepdims=True)
        un = dot(wn.astype(BF16), nv_ref[new, :])
        weights = [jnp.exp2((scores[i] - tops[i]) * scale) for i in range(many)]
        summed = [dot(weights[i].astype(BF16), sv[first + i]) for i in range(many)]
        for i in range(many):
            total = jnp.sum(weights[i], axis=-1, keepdims=True) + total_n[half[i]]
            own_a[first + i] = (summed[i] + un[half[i]]) / total
            own_l[first + i] = jnp.broadcast_to(tops[i] * scale + jnp.log(total) * LOG2E, (heads, width))

    load_nk.wait()
    load_nv.wait()

    def local_chunk(c, _):
        for copy in suffix_copies(c):
            copy.wait()

        def one(i, _):
            local(c * (step // many) + i)
            return 0

        lax.fori_loop(0, step // many, one, 0)
        return 0

    lax.fori_loop(0, early, local_chunk, 0)

    def serve(i, _):
        source = source_of(me, turn(i, n), n)
        q_copy(source, source).wait_recv()
        attend(source)
        t_copy(source, me).start()
        r_copy(source, me).start()
        return 0

    lax.fori_loop(1, n, serve, 0)
    lax.fori_loop(early, chunks, local_chunk, 0)

    r_recv[me] = r_send[me]
    t_recv[me] = t_send[me]

    shared = (cap // fold, heads, width)
    spread = lax.broadcasted_iota(jnp.int32, shared, 2) - lax.broadcasted_iota(jnp.int32, shared, 1)

    def widen(owner):
        stat = t_recv[owner]
        levels = []
        for f in range(fold):
            level = jnp.sum(jnp.where(spread == f * heads, stat, 0.0), axis=2, keepdims=True)
            levels.append(jnp.broadcast_to(level, shared).reshape(cap // fold, 1, heads, width))
        joined = jnp.concatenate(levels, axis=1) if fold > 1 else levels[0]
        level_ref[owner] = joined.reshape(cap, heads, width)

    widen(me)

    def finish(i, _):
        peer = partner(me, turn(i, n), n)
        t_copy(peer, peer).wait_recv()
        widen(peer)
        r_copy(peer, peer).wait_recv()
        return 0

    lax.fori_loop(1, n, finish, 0)

    def out_copy(c):
        part = pl.ds(c * step, step)
        return pltpu.make_async_copy(out_ref.at[part], out_hbm.at[part], o_sem.at[c])

    def merge_chunk(c, _):
        def merge(index, _):
            first = c * step + index * many
            results = []
            for i in range(many):
                slot = places[0, first + i]
                owner, rank = slot // cap, lax.rem(slot, cap)
                a1 = r_recv[owner, rank].astype(F32)
                share = 1.0 / (1.0 + jnp.exp2(own_l[first + i] - level_ref[owner, rank]))
                a2 = own_a[first + i]
                results.append((a2 + (a1 - a2) * share).astype(BF16))
            for i in range(many):
                out_ref[first + i] = results[i]
            return 0

        lax.fori_loop(0, step // many, merge, 0)
        out_copy(c).start()
        return 0

    lax.fori_loop(0, chunks, merge_chunk, 0)

    def drain_out(c, _):
        out_copy(c).wait()
        return 0

    lax.fori_loop(0, chunks, drain_out, 0)

    def drain(k, _):
        peer = lax.rem(me + k, n)
        q_copy(peer, me).wait_send()
        r_copy(peer, me).wait_send()
        t_copy(peer, me).wait_send()
        return 0

    lax.fori_loop(1, n, drain, 0)


def on_device(
    n,
    queries,
    new_keys,
    new_values,
    suffix_keys,
    suffix_values,
    suffix_lengths,
    prefix_ids,
    prefix_owner,
    prefix_keys,
    prefix_values,
):
    rows, steps, head_count, width = queries.shape
    kvs = new_keys.shape[2]
    heads = steps * head_count
    slen = suffix_keys.shape[1]
    plen = prefix_keys.shape[1]
    cap = max(2, 2 * rows // n)
    chunks = 4
    fold = math.gcd(cap, max(1, width // heads))
    smem = pl.BlockSpec(memory_space=pltpu.SMEM)
    vmem = pl.BlockSpec(memory_space=pltpu.VMEM)
    hbm = pl.BlockSpec(memory_space=pl.ANY)

    flops = 4 * n * cap * heads * plen * width + 4 * rows * heads * kvs * slen * width
    out = pl.pallas_call(
        functools.partial(kernel, n, cap, kvs, steps, steps * kvs, chunks),
        out_shape=jax.ShapeDtypeStruct((rows, heads, width), BF16),
        in_specs=[vmem, smem, smem, hbm, hbm, hbm, hbm, hbm, hbm, hbm],
        out_specs=hbm,
        scratch_shapes=[
            pltpu.VMEM((2, n * cap), jnp.int32),
            pltpu.SMEM((2, n * cap), jnp.int32),
            pltpu.VMEM((rows * steps * kvs, width), BF16),
            pltpu.VMEM((rows * steps * kvs, width), BF16),
            pltpu.VMEM((rows, heads, width), BF16),
            pltpu.VMEM((n, cap, heads, width), F32),
            pltpu.VMEM((rows, heads, width), BF16),
            pltpu.VMEM((n, cap, heads, width), BF16),
            pltpu.VMEM((n, cap, heads, width), BF16),
            pltpu.VMEM((n, cap, heads, width), BF16),
            pltpu.VMEM((n, cap, heads, width), BF16),
            pltpu.VMEM((n, cap // fold, 1, width), F32),
            pltpu.VMEM((n, cap // fold, 1, width), F32),
            pltpu.VMEM((2, plen * kvs, width), BF16),
            pltpu.VMEM((256 * kvs, width), F32),
            pltpu.VMEM((kvs, plen, width), BF16),
            pltpu.VMEM((kvs, plen, 2 * width), BF16),
            pltpu.VMEM((rows, slen * kvs, width), BF16),
            pltpu.VMEM((rows, slen * kvs, width), BF16),
            pltpu.VMEM((rows, heads, width), F32),
            pltpu.VMEM((rows, heads, width), F32),
            pltpu.SemaphoreType.DMA,
            pltpu.SemaphoreType.DMA((2,)),
            pltpu.SemaphoreType.DMA((chunks,)),
            pltpu.SemaphoreType.DMA,
            pltpu.SemaphoreType.DMA((2,)),
            pltpu.SemaphoreType.DMA((2, chunks)),
            pltpu.SemaphoreType.DMA((n,)),
            pltpu.SemaphoreType.DMA((n,)),
            pltpu.SemaphoreType.DMA((n,)),
            pltpu.SemaphoreType.DMA((n,)),
            pltpu.SemaphoreType.DMA((n,)),
            pltpu.SemaphoreType.DMA((n,)),
        ],
        compiler_params=pltpu.CompilerParams(
            collective_id=0, has_side_effects=True, vmem_limit_bytes=58 * 1024 * 1024
        ),
        cost_estimate=pl.CostEstimate(
            flops=flops, bytes_accessed=24 * 1024 * 1024, transcendentals=n * cap * heads * plen
        ),
    )(
        prefix_ids.reshape(1, rows),
        prefix_owner,
        suffix_lengths,
        queries.reshape(rows, heads, width),
        new_keys.reshape(rows * steps * kvs, width),
        new_values.reshape(rows * steps * kvs, width),
        suffix_keys.reshape(rows, slen * kvs, width),
        suffix_values.reshape(rows, slen * kvs, width),
        prefix_keys.reshape(plen * kvs, width),
        prefix_values.reshape(plen * kvs, width),
    )
    return out.reshape(queries.shape)


def solution(mesh):
    in_specs = (
        P("dp", None, "tp", None),
        P("dp", None, "tp", None),
        P("dp", None, "tp", None),
        P("dp", None, "tp", None),
        P("dp", None, "tp", None),
        P("dp"),
        P("dp", None),
        P(),
        P("dp", None, "tp", None),
        P("dp", None, "tp", None),
    )
    out_specs = P("dp", None, "tp", None)
    return jax.shard_map(
        functools.partial(on_device, mesh.shape["dp"]),
        mesh=mesh,
        in_specs=in_specs,
        out_specs=out_specs,
        check_vma=False,
    )
```
